32 devices in a mesh: groups: 2 (over y), seq: 16 (over z, x, core).
Axes of the slice: x: 2, y: 2, z: 4, core: 2. Of those that a mesh axis runs over, the one named last changes fastest.
Arguments:
- query_src: bfloat16 [4096, 2048], P(('groups', 'seq')), parts along dimension 0, may hold values from -6 to 6
- key_src: bfloat16 [4096, 2048], P(('groups', 'seq')), parts along dimension 0, may hold values from -6 to 6
- value_src: bfloat16 [4096, 2048], P(('groups', 'seq')), parts along dimension 0, may hold values from -6 to 6
- up_query: bfloat16 [4096, 2048], P(('groups', 'seq')), parts along dimension 0, may hold values from -6 to 6
- query_gain: float32 [2048], replicated, may hold values from 1.2 to 2.4
- key_gain: float32 [2048], replicated, may hold values from 1.2 to 2.4
- up_gain: float32 [2048], replicated, may hold values from 1.5 to 5
Outputs:
- upsampled: bfloat16 [4096, 2048], P(('groups', 'seq')), parts along dimension 0
The draws below stay inside these ranges and needn't reach their ends.
There are 2 independent parts, one for each index of `groups`. The reference program is written for one: setup_inputs(seed, part) draws one part's arguments, and reference() takes and returns one part's arrays. A program takes and returns all parts, laid end to end along the dimension named above; an argument that names none is the same for every part. Nothing has to cross between parts.
All inputs are finite; a program needn't handle non-finite values.
Results may differ from the reference program's by a relative error of at most 0.002.
The reference program's roundings to bfloat16 on the way count: a program that leaves them out, or rounds other values in their place, can miss the bound.
Values may be sent and summed in bfloat16 or wider, within the bound.
A program may use at most 128 MiB of HBM per device.

```python
import math
import jax
import jax.numpy as jnp
from jax import lax

HEADS = 16
HDIM = 128
SHORT = 4
SHIFT = 3
HD = 2048
TOKENS = 2048


def block_scale(key, extent, cuts, low, largest):
    def one(axis_at, parts):
        draws = jax.random.uniform(jax.random.fold_in(jax.random.fold_in(key, 6), axis_at), (parts,), jnp.float32, low / len(cuts), largest / len(cuts))
        return jnp.repeat(jnp.exp(draws), extent[axis_at] // parts).reshape((-1,) + (1,) * (len(extent) - axis_at - 1))

    level = one(*cuts[0])
    for cut in cuts[1:]:
        level = level * one(*cut)
    return level


def normal_values(key, extent, deviation, limit, cuts=(), dtype=jnp.bfloat16):
    entries = deviation * jax.random.normal(key, extent, jnp.float32)
    if cuts:
        entries = entries * block_scale(key, extent, cuts, -0.22, 0.18)
    return jnp.clip(entries, -limit, limit).astype(dtype)


def setup_inputs(seed: int = 0, part: int = 0) -> dict:
    arg_keys = jax.random.split(jax.random.key(seed), 8)
    part_keys = jax.random.split(jax.random.fold_in(arg_keys[7], part), 8)
    return {
        "query_src": normal_values(part_keys[0], (TOKENS, HD), 1.0, 6.0, ((0, 16),)),
        "key_src": normal_values(part_keys[1], (TOKENS, HD), 1.0, 6.0, ((0, 16),)),
        "value_src": normal_values(part_keys[2], (TOKENS, HD), 1.0, 6.0, ((0, 16),)),
        "up_query": normal_values(part_keys[3], (TOKENS, HD), 1.0, 6.0, ((0, 16),)),
        "query_gain": jnp.clip(jnp.exp(jax.random.uniform(arg_keys[4], (HD,), jnp.float32, math.log(1.2), math.log(2.4))), 1.2, 2.4),
        "key_gain": jnp.clip(jnp.exp(jax.random.uniform(arg_keys[5], (HD,), jnp.float32, math.log(1.2), math.log(2.4))), 1.2, 2.4),
        "up_gain": jnp.clip(jnp.exp(jax.random.uniform(arg_keys[6], (HD,), jnp.float32, math.log(1.5), math.log(5.0))), 1.5, 5.0),
    }


epsilon = 1e-06

def head_norm(values, gain_vector):
    row_count = values.shape[0]
    by_head = values.reshape(row_count, HEADS, HDIM)
    inverse_rms = lax.rsqrt(lax.optimization_barrier(jnp.mean(by_head * by_head, axis=2, keepdims=True)) + epsilon)
    return (by_head * inverse_rms * gain_vector.reshape(1, HEADS, HDIM)).reshape(row_count, HEADS * HDIM)

def pool_rows(source):
    widened = source.astype(jnp.float32)
    width = widened.shape[1]
    shifted = jnp.concatenate([jnp.zeros((SHIFT, width), jnp.float32), widened[:widened.shape[0] - SHIFT]], axis=0)
    return lax.optimization_barrier(jnp.mean(shifted.reshape(-1, SHORT, width), axis=1))

def attend_rows(queries, key_rows, value_rows, visible):
    scores = jnp.dot(queries, key_rows.T, preferred_element_type=jnp.float32) / math.sqrt(HDIM)
    exponent = jnp.where(visible, jnp.exp(scores), 0.0)
    denominator = lax.optimization_barrier(jnp.sum(exponent, axis=1, keepdims=True))
    numerator = jnp.dot(exponent.astype(jnp.bfloat16), value_rows, preferred_element_type=jnp.float32)
    return numerator / denominator

def split_heads(matrix, length):
    return jnp.transpose(matrix.reshape(length, HEADS, HDIM), (1, 0, 2))

def reference(query_src, key_src, value_src, up_query, query_gain, key_gain, up_gain):
    short_query = head_norm(pool_rows(query_src), query_gain).astype(jnp.bfloat16)
    short_key = head_norm(pool_rows(key_src), key_gain).astype(jnp.bfloat16)
    short_value = pool_rows(value_src).astype(jnp.bfloat16)
    row_count = short_query.shape[0]
    token_count = up_query.shape[0]
    row_pos = jnp.arange(row_count)
    short_visible = row_pos[None, :] <= row_pos[:, None]

    def short_head(operands):
        head_query, head_key, head_value = operands
        attended = attend_rows(head_query, head_key, head_value, short_visible)
        inverse_rms = lax.rsqrt(lax.optimization_barrier(jnp.mean(attended * attended, axis=1, keepdims=True)) + epsilon)
        return (attended * inverse_rms).astype(jnp.bfloat16)
    memory = lax.map(short_head, (split_heads(short_query, row_count), split_heads(short_key, row_count), split_heads(short_value, row_count)))
    up_heads = split_heads(head_norm(up_query.astype(jnp.float32), up_gain).astype(jnp.bfloat16), token_count)
    token_block = token_count // 8
    row_block = row_count // 8
    pieces = []
    for block_index in range(8):
        key_count = (block_index + 1) * row_block
        tok_pos = jnp.arange(block_index * token_block, (block_index + 1) * token_block)
        visible = jnp.arange(key_count)[None, :] * SHORT <= tok_pos[:, None]
        query_part = up_heads[:, block_index * token_block:(block_index + 1) * token_block]

        def up_head(operands, visible=visible, key_count=key_count):
            head_query, head_memory = operands
            return attend_rows(head_query, head_memory[:key_count], head_memory[:key_count], visible)
        pieces.append(lax.map(up_head, (query_part, memory)))
    combined = jnp.concatenate(pieces, axis=1)
    return jnp.transpose(combined, (1, 0, 2)).reshape(token_count, HEADS * HDIM).astype(jnp.bfloat16)
```

```python
import functools
import math

import jax
import jax.numpy as jnp
from jax import lax
from jax.experimental import pallas as pl
from jax.experimental.pallas import tpu as pltpu
from jax.sharding import PartitionSpec as P

HEADS = 16
HDIM = 128
SHORT = 4
SHIFT = 3


epsilon = 1e-06


def shifted(value, axis, steps):
    count = lax.axis_size(axis)
    leading, last = (max(0, -steps), min(count, count - steps))
    return lax.ppermute(value, axis, [(source, source + steps) for source in range(leading, last)])


def head_norm(values, gain_vector):
    row_count = values.shape[0]
    by_head = values.reshape(row_count, HEADS, HDIM)
    inverse_rms = lax.rsqrt(jnp.mean(by_head * by_head, axis=2, keepdims=True) + epsilon)
    return (by_head * inverse_rms * gain_vector.reshape(1, HEADS, HDIM)).reshape(
        row_count, HEADS * HDIM
    )


def row_norm(values):
    return values * lax.rsqrt(jnp.mean(values * values, axis=-1, keepdims=True) + epsilon)


def pooled_rows(source, edge_rows):
    widened = jnp.concatenate([edge_rows, source[: source.shape[0] - SHIFT]], axis=0).astype(
        jnp.float32
    )
    return jnp.mean(widened.reshape(-1, SHORT, widened.shape[1]), axis=1)


def blocked_attention(queries, query_limit, key_rows, value_rows, key_positions, block_size):
    head_count, query_count, head_size = queries.shape
    block_total = key_rows.shape[1] // block_size
    ceiling = jnp.max(query_limit)

    def visit_block(block_index, totals):
        offset = block_index * block_size
        block_pos = lax.dynamic_slice_in_dim(key_positions, offset, block_size, 0)

        def compute(state):
            numer_in, denom_in = state
            key_block = lax.dynamic_slice_in_dim(key_rows, offset, block_size, 1)
            value_block = lax.dynamic_slice_in_dim(value_rows, offset, block_size, 1)
            scores = jnp.einsum(
                "hqd,hkd->hqk", queries, key_block, preferred_element_type=jnp.float32
            ) / math.sqrt(HDIM)
            visible = block_pos[None, :] <= query_limit[:, None]
            exponent = jnp.where(visible[None], jnp.exp(scores), 0.0)
            denom_out = denom_in + jnp.sum(exponent, axis=2)
            numer_out = numer_in + jnp.einsum(
                "hqk,hkd->hqd",
                exponent.astype(jnp.bfloat16),
                value_block,
                preferred_element_type=jnp.float32,
            )
            return (numer_out, denom_out)

        return lax.cond(jnp.min(block_pos) <= ceiling, compute, lambda state: state, totals)

    initial = (
        jnp.zeros((head_count, query_count, head_size), jnp.float32),
        jnp.zeros((head_count, query_count), jnp.float32),
    )
    numerator, denominator = lax.fori_loop(0, block_total, visit_block, initial)
    return numerator / denominator[:, :, None]


def spread_heads(matrices, row_count, block_count, device_count):
    count = len(matrices)
    joined = jnp.stack(matrices).reshape(count, row_count, HEADS, HDIM)
    joined = jnp.transpose(joined, (2, 0, 1, 3)).reshape(HEADS, 1, count * row_count, HDIM)
    return jnp.broadcast_to(joined, (HEADS, block_count, count * row_count, HDIM)).reshape(
        device_count, count * row_count, HDIM
    )


def split_pieces(matrix, row_count, block_count, device_count):
    piece = row_count // block_count
    parted = matrix.reshape(block_count, piece, HEADS, HDIM)
    return jnp.transpose(parted, (2, 0, 1, 3)).reshape(device_count, piece, HDIM)


def local_general(query_src, key_src, value_src, up_query, query_gain, key_gain, up_gain):
    device_count = lax.axis_size("seq")
    device_index = lax.axis_index("seq")
    block_count = device_count // HEADS
    block_index = device_index % block_count
    token_count = query_src.shape[0]
    edges = jnp.stack(
        [
            query_src[token_count - SHIFT :],
            key_src[token_count - SHIFT :],
            value_src[token_count - SHIFT :],
        ]
    )
    edges = shifted(edges, "seq", 1)
    short_query = head_norm(pooled_rows(query_src, edges[0]), query_gain).astype(jnp.bfloat16)
    short_key = head_norm(pooled_rows(key_src, edges[1]), key_gain).astype(jnp.bfloat16)
    short_value = pooled_rows(value_src, edges[2]).astype(jnp.bfloat16)
    row_count = short_query.shape[0]
    up_heads = head_norm(up_query.astype(jnp.float32), up_gain).astype(jnp.bfloat16)
    row_total = row_count * device_count
    key_block = math.gcd(512, row_total)
    row_positions = jnp.arange(row_total, dtype=jnp.int32)
    device_rows = jnp.arange(device_count, dtype=jnp.int32)[:, None]
    qkv_out = spread_heads(
        [short_query, short_key, short_value], row_count, block_count, device_count
    )
    up_out = split_pieces(up_heads, token_count, block_count, device_count)
    arrived, own_up = (
        lax.all_to_all(qkv_out, "seq", split_axis=0, concat_axis=0, tiled=True),
        lax.all_to_all(up_out, "seq", split_axis=0, concat_axis=0, tiled=True),
    )
    all_query = arrived[:, :row_count].reshape(row_total, HDIM)
    all_key = arrived[:, row_count : 2 * row_count].reshape(row_total, HDIM)
    all_value = arrived[:, 2 * row_count :].reshape(row_total, HDIM)

    def fill_block(index_now, memory_now):
        offset = index_now * key_block
        block_query = lax.dynamic_slice_in_dim(all_query, offset, key_block, 0)[None]
        limits = offset + jnp.arange(key_block, dtype=jnp.int32)
        attended = blocked_attention(
            block_query, limits, all_key[None], all_value[None], row_positions, key_block
        )[0]
        return lax.dynamic_update_slice_in_dim(
            memory_now, row_norm(attended).astype(jnp.bfloat16), offset, 0
        )

    memory = lax.fori_loop(
        0, row_total // key_block, fill_block, jnp.zeros((row_total, HDIM), jnp.bfloat16)
    )
    token_piece = token_count // block_count
    own_tokens = (
        device_rows * token_count
        + block_index * token_piece
        + jnp.arange(token_piece, dtype=jnp.int32)[None, :]
    ).reshape(-1)
    own_up = own_up.reshape(1, device_count * token_piece, HDIM)
    result = blocked_attention(
        own_up, own_tokens // SHORT, memory[None], memory[None], row_positions, key_block
    )[0]
    result = result.astype(jnp.bfloat16).reshape(device_count, token_piece, HDIM)
    returned = lax.all_to_all(result, "seq", split_axis=0, concat_axis=0, tiled=True)
    output_heads = returned.reshape(HEADS, token_count, HDIM)
    return jnp.transpose(output_heads, (1, 0, 2)).reshape(token_count, HEADS * HDIM)


NT = (((1,), (1,)), ((), ()))


def attend(queries, keys, values, first_row, tokens_per_row, masked_from):
    scores = lax.dot_general(queries, keys, NT, preferred_element_type=jnp.float32)
    exponent = jnp.exp(scores * (1.0 / math.sqrt(HDIM)))
    last = exponent[:, masked_from:]
    row = lax.broadcasted_iota(jnp.int32, last.shape, 0) + first_row
    key = lax.broadcasted_iota(jnp.int32, last.shape, 1) * tokens_per_row
    last = jnp.where(key <= row, last, 0.0)
    parts = [last]
    if masked_from:
        parts = [exponent[:, :masked_from], last]
    exponent = jnp.concatenate(parts, axis=1) if masked_from else last
    denominator = jnp.sum(exponent, axis=1, keepdims=True)
    numerator = jnp.dot(
        exponent.astype(jnp.bfloat16), values, preferred_element_type=jnp.float32
    )
    return numerator / denominator


def fused_kernel(
    n, team, planes,
    query_src, key_src, value_src, up_query, query_gain, key_gain, up_gain,
    out_ref,
    edge_send, edge_recv, up_send, up_recv, qkv_send, qkv_recv, mem, ret_send,
    edge_sems, up_ssem, up_rsem, qkv_ssem, qkv_rsem, mem_ssem, mem_rsem, ret_ssem, ret_rsem,
    local_sems,
):
    me = lax.axis_index("seq")
    plane = me // team
    member = me % team
    tokens = query_src.shape[0]
    rows = tokens // SHORT
    block = rows * team

    def remote(src, dst, ssem, rsem, target):
        return pltpu.make_async_remote_copy(
            src_ref=src, dst_ref=dst, send_sem=ssem, recv_sem=rsem,
            device_id={"seq": target}, device_id_type=pl.DeviceIdType.MESH,
        )

    barrier = pltpu.get_barrier_semaphore()

    @pl.loop(1, n)
    def _(k):
        pl.semaphore_signal(
            barrier, inc=1, device_id={"seq": (me + k) % n},
            device_id_type=pl.DeviceIdType.MESH,
        )

    sources = (query_src, key_src, value_src)
    edge_token = lax.broadcasted_iota(jnp.int32, (8, tokens), 1)
    edge_row = lax.broadcasted_iota(jnp.int32, (8, tokens), 0)
    edge = None
    for at, source in enumerate(sources):
        pick = jnp.where(
            (edge_row == at) & (edge_token >= tokens - SHIFT), 1.0 / SHORT, 0.0
        ).astype(jnp.bfloat16)
        term = jnp.dot(pick, source[...], preferred_element_type=jnp.float32)
        edge = term if edge is None else edge + term
    edge_send[...] = edge
    pl.semaphore_wait(barrier, n - 1)

    edge_copy = remote(
        edge_send, edge_recv, edge_sems.at[0], edge_sems.at[1], lax.min(me + 1, n - 1)
    )

    @pl.when(me < n - 1)
    def _():
        edge_copy.start()

    for head in range(HEADS):
        cols = slice(head * HDIM, (head + 1) * HDIM)
        part = up_query[:, cols].astype(jnp.float32)
        scale = lax.rsqrt(jnp.mean(part * part, axis=1, keepdims=True) + epsilon)
        up_send[head] = (part * scale * up_gain[:, cols]).astype(jnp.bfloat16)

    edge_recv_zero = me == 0

    @pl.when(edge_recv_zero)
    def _():
        edge_recv[...] = jnp.zeros_like(edge_recv)

    @pl.when(me > 0)
    def _():
        edge_copy.wait_recv()

    pool_row = lax.broadcasted_iota(jnp.int32, (rows, tokens), 0) * SHORT
    pool_token = lax.broadcasted_iota(jnp.int32, (rows, tokens), 1)
    pool = jnp.where(
        (pool_token <= pool_row) & (pool_token >= pool_row - SHIFT), 1.0 / SHORT, 0.0
    ).astype(jnp.bfloat16)
    first = lax.broadcasted_iota(jnp.int32, (rows, HDIM), 0) == 0
    for at, (source, gain) in enumerate(zip(sources, (query_gain, key_gain, None))):
        pooled = jnp.dot(pool, source[...], preferred_element_type=jnp.float32)
        for head in range(HEADS):
            cols = slice(head * HDIM, (head + 1) * HDIM)
            part = pooled[:, cols]
            part = part + jnp.where(first, edge_recv[at : at + 1, cols], 0.0)
            if gain is not None:
                scale = lax.rsqrt(jnp.mean(part * part, axis=1, keepdims=True) + epsilon)
                part = part * scale * gain[:, cols]
            qkv_send[head, at * rows : (at + 1) * rows] = part.astype(jnp.bfloat16)

    def head_of(device):
        return (device % team) * planes + device // team

    def qkv_copy(target):
        return remote(
            qkv_send.at[head_of(target)], qkv_recv.at[me],
            qkv_ssem.at[target], qkv_rsem.at[me], target,
        )

    @pl.loop(1, n)
    def _(k):
        qkv_copy((me + k) % n).start()

    def up_copy(target):
        return remote(
            up_send.at[pl.ds(target * planes, planes)], up_recv.at[member],
            up_ssem.at[target], up_rsem.at[member], plane * team + target,
        )

    @pl.loop(1, team)
    def _(k):
        up_copy((member + k) % team).start()

    own_qkv = pltpu.make_async_copy(
        qkv_send.at[head_of(me)], qkv_recv.at[me], local_sems.at[0]
    )
    own_up = pltpu.make_async_copy(
        up_send.at[pl.ds(member * planes, planes)], up_recv.at[member], local_sems.at[1]
    )
    own_qkv.start()
    own_up.start()
    own_qkv.wait()

    def mem_copy(target, at):
        part = mem.at[plane, at * block : (at + 1) * block]
        return remote(
            part, part, mem_ssem.at[target, at], mem_rsem.at[plane, at],
            target * team + member,
        )

    for at in range(planes):
        for other in range(team):
            source = at * team + other

            @pl.when(source != me)
            def _():
                remote(
                    qkv_send.at[0], qkv_recv.at[source],
                    qkv_ssem.at[source], qkv_rsem.at[source], source,
                ).wait_recv()

        upto = (at + 1) * team
        queries = qkv_recv[at * team : upto, :rows].reshape(block, HDIM)
        keys = qkv_recv[:upto, rows : 2 * rows].reshape(upto * rows, HDIM)
        values = qkv_recv[:upto, 2 * rows :].reshape(upto * rows, HDIM)
        attended = attend(queries, keys, values, 0, 1, at * block)
        mem[plane, at * block : (at + 1) * block] = row_norm(attended).astype(jnp.bfloat16)
        for target in reversed(range(at, planes)):

            @pl.when(target != plane)
            def _():
                mem_copy(target, at).start()

    own_up.wait()

    @pl.loop(1, team)
    def _(k):
        source = (member + k) % team
        remote(
            up_send.at[pl.ds(0, planes)], up_recv.at[source],
            up_ssem.at[source], up_rsem.at[source], plane * team + source,
        ).wait_recv()

    def ret_copy(target, part):
        column = pl.multiple_of((member * planes + part) * HDIM, HDIM)
        return remote(
            ret_send.at[target, part], out_ref.at[:, pl.ds(column, HDIM)],
            ret_ssem.at[target, part], ret_rsem.at[member, part], plane * team + target,
        )

    for here in range(planes):

        @pl.when(plane == here)
        def _():
            count = (here + 1) * block

            @pl.loop(0, planes)
            def _(step):
                part = (here + step) % planes

                @pl.when(part != here)
                def _():
                    for at in range(here + 1):
                        slot = mem.at[part, at * block : (at + 1) * block]
                        remote(
                            slot, slot, mem_ssem.at[part, at], mem_rsem.at[part, at],
                            part * team + member,
                        ).wait_recv()

                memory = mem[part, :count]
                for target in range(team):
                    value = attend(
                        up_recv[target, part], memory, memory,
                        target * tokens, SHORT, here * block,
                    ).astype(jnp.bfloat16)
                    ret_send[target, part] = value

                for target in range(team):

                    @pl.when(target != member)
                    def _():
                        ret_copy(target, part).start()

                column = pl.multiple_of((member * planes + part) * HDIM, HDIM)
                out_ref[:, pl.ds(column, HDIM)] = ret_send[member, part]

    @pl.when(me < n - 1)
    def _():
        edge_copy.wait_send()

    @pl.loop(1, n)
    def _(k):
        qkv_copy((me + k) % n).wait_send()

    @pl.loop(1, team)
    def _(k):
        up_copy((member + k) % team).wait_send()

    for at in range(planes):
        for target in range(at, planes):

            @pl.when(target != plane)
            def _():
                mem_copy(target, at).wait_send()

    @pl.loop(1, team)
    def _(k):
        other = (member + k) % team
        for part in range(planes):
            ret_copy(other, part).wait_send()
            column = pl.multiple_of((other * planes + part) * HDIM, HDIM)
            remote(
                ret_send.at[other, part], out_ref.at[:, pl.ds(column, HDIM)],
                ret_ssem.at[other, part], ret_rsem.at[other, part], plane * team + other,
            ).wait_recv()


def local_fused(query_src, key_src, value_src, up_query, query_gain, key_gain, up_gain):
    n = lax.axis_size("seq")
    team = math.isqrt(n)
    planes = n // team
    tokens, width = query_src.shape
    rows = tokens // SHORT
    bf16, dma = jnp.bfloat16, pltpu.SemaphoreType.DMA
    return pl.pallas_call(
        functools.partial(fused_kernel, n, team, planes),
        out_shape=jax.ShapeDtypeStruct((tokens, width), bf16),
        in_specs=[pl.BlockSpec(memory_space=pltpu.VMEM)] * 7,
        out_specs=pl.BlockSpec(memory_space=pltpu.VMEM),
        scratch_shapes=[
            pltpu.VMEM((8, width), jnp.float32),
            pltpu.VMEM((8, width), jnp.float32),
            pltpu.VMEM((HEADS, tokens, HDIM), bf16),
            pltpu.VMEM((team, planes, tokens, HDIM), bf16),
            pltpu.VMEM((HEADS, 3 * rows, HDIM), bf16),
            pltpu.VMEM((n, 3 * rows, HDIM), bf16),
            pltpu.VMEM((planes, n * rows, HDIM), bf16),
            pltpu.VMEM((team, planes, tokens, HDIM), bf16),
            dma((2,)),
            dma((team,)),
            dma((team,)),
            dma((n,)),
            dma((n,)),
            dma((planes, planes)),
            dma((planes, planes)),
            dma((team, planes)),
            dma((team, planes)),
            dma((2,)),
        ],
        compiler_params=pltpu.CompilerParams(
            collective_id=0, has_side_effects=True, vmem_limit_bytes=48 * 1024 * 1024
        ),
    )(
        query_src, key_src, value_src, up_query,
        query_gain.reshape(1, width), key_gain.reshape(1, width), up_gain.reshape(1, width),
    )


def local(query_src, *others):
    n = lax.axis_size("seq")
    square = math.isqrt(n) ** 2 == n
    whole_tiles = query_src.shape[0] % (16 * SHORT) == 0
    if n == HEADS and square and whole_tiles:
        return local_fused(query_src, *others)
    return local_general(query_src, *others)


def solution(mesh):
    in_specs = (
        P(("groups", "seq"), None),
        P(("groups", "seq"), None),
        P(("groups", "seq"), None),
        P(("groups", "seq"), None),
        P(),
        P(),
        P(),
    )
    out_specs = P(("groups", "seq"), None)
    return jax.shard_map(local, mesh=mesh, in_specs=in_specs, out_specs=out_specs, check_vma=False)
```

```python
import functools
import math

import jax
import jax.numpy as jnp
from jax import lax
from jax.experimental import pallas as pl
from jax.experimental.pallas import tpu as pltpu
from jax.sharding import PartitionSpec as P

HEADS = 16
HDIM = 128
SHORT = 4
SHIFT = 3


epsilon = 1e-06


def shifted(value, axis, steps):
    count = lax.axis_size(axis)
    leading, last = (max(0, -steps), min(count, count - steps))
    return lax.ppermute(value, axis, [(source, source + steps) for source in range(leading, last)])


def head_norm(values, gain_vector):
    row_count = values.shape[0]
    by_head = values.reshape(row_count, HEADS, HDIM)
    inverse_rms = lax.rsqrt(jnp.mean(by_head * by_head, axis=2, keepdims=True) + epsilon)
    return (by_head * inverse_rms * gain_vector.reshape(1, HEADS, HDIM)).reshape(
        row_count, HEADS * HDIM
    )


def row_norm(values):
    return values * lax.rsqrt(jnp.mean(values * values, axis=-1, keepdims=True) + epsilon)


def pooled_rows(source, edge_rows):
    widened = jnp.concatenate([edge_rows, source[: source.shape[0] - SHIFT]], axis=0).astype(
        jnp.float32
    )
    return jnp.mean(widened.reshape(-1, SHORT, widened.shape[1]), axis=1)


def blocked_attention(queries, query_limit, key_rows, value_rows, key_positions, block_size):
    head_count, query_count, head_size = queries.shape
    block_total = key_rows.shape[1] // block_size
    ceiling = jnp.max(query_limit)

    def visit_block(block_index, totals):
        offset = block_index * block_size
        block_pos = lax.dynamic_slice_in_dim(key_positions, offset, block_size, 0)

        def compute(state):
            numer_in, denom_in = state
            key_block = lax.dynamic_slice_in_dim(key_rows, offset, block_size, 1)
            value_block = lax.dynamic_slice_in_dim(value_rows, offset, block_size, 1)
            scores = jnp.einsum(
                "hqd,hkd->hqk", queries, key_block, preferred_element_type=jnp.float32
            ) / math.sqrt(HDIM)
            visible = block_pos[None, :] <= query_limit[:, None]
            exponent = jnp.where(visible[None], jnp.exp(scores), 0.0)
            denom_out = denom_in + jnp.sum(exponent, axis=2)
            numer_out = numer_in + jnp.einsum(
                "hqk,hkd->hqd",
                exponent.astype(jnp.bfloat16),
                value_block,
                preferred_element_type=jnp.float32,
            )
            return (numer_out, denom_out)

        return lax.cond(jnp.min(block_pos) <= ceiling, compute, lambda state: state, totals)

    initial = (
        jnp.zeros((head_count, query_count, head_size), jnp.float32),
        jnp.zeros((head_count, query_count), jnp.float32),
    )
    numerator, denominator = lax.fori_loop(0, block_total, visit_block, initial)
    return numerator / denominator[:, :, None]


def spread_heads(matrices, row_count, block_count, device_count):
    count = len(matrices)
    joined = jnp.stack(matrices).reshape(count, row_count, HEADS, HDIM)
    joined = jnp.transpose(joined, (2, 0, 1, 3)).reshape(HEADS, 1, count * row_count, HDIM)
    return jnp.broadcast_to(joined, (HEADS, block_count, count * row_count, HDIM)).reshape(
        device_count, count * row_count, HDIM
    )


def split_pieces(matrix, row_count, block_count, device_count):
    piece = row_count // block_count
    parted = matrix.reshape(block_count, piece, HEADS, HDIM)
    return jnp.transpose(parted, (2, 0, 1, 3)).reshape(device_count, piece, HDIM)


def local_general(query_src, key_src, value_src, up_query, query_gain, key_gain, up_gain):
    device_count = lax.axis_size("seq")
    device_index = lax.axis_index("seq")
    block_count = device_count // HEADS
    block_index = device_index % block_count
    token_count = query_src.shape[0]
    edges = jnp.stack(
        [
            query_src[token_count - SHIFT :],
            key_src[token_count - SHIFT :],
            value_src[token_count - SHIFT :],
        ]
    )
    edges = shifted(edges, "seq", 1)
    short_query = head_norm(pooled_rows(query_src, edges[0]), query_gain).astype(jnp.bfloat16)
    short_key = head_norm(pooled_rows(key_src, edges[1]), key_gain).astype(jnp.bfloat16)
    short_value = pooled_rows(value_src, edges[2]).astype(jnp.bfloat16)
    row_count = short_query.shape[0]
    up_heads = head_norm(up_query.astype(jnp.float32), up_gain).astype(jnp.bfloat16)
    row_total = row_count * device_count
    key_block = math.gcd(512, row_total)
    row_positions = jnp.arange(row_total, dtype=jnp.int32)
    device_rows = jnp.arange(device_count, dtype=jnp.int32)[:, None]
    qkv_out = spread_heads(
        [short_query, short_key, short_value], row_count, block_count, device_count
    )
    up_out = split_pieces(up_heads, token_count, block_count, device_count)
    arrived, own_up = (
        lax.all_to_all(qkv_out, "seq", split_axis=0, concat_axis=0, tiled=True),
        lax.all_to_all(up_out, "seq", split_axis=0, concat_axis=0, tiled=True),
    )
    all_query = arrived[:, :row_count].reshape(row_total, HDIM)
    all_key = arrived[:, row_count : 2 * row_count].reshape(row_total, HDIM)
    all_value = arrived[:, 2 * row_count :].reshape(row_total, HDIM)

    def fill_block(index_now, memory_now):
        offset = index_now * key_block
        block_query = lax.dynamic_slice_in_dim(all_query, offset, key_block, 0)[None]
        limits = offset + jnp.arange(key_block, dtype=jnp.int32)
        attended = blocked_attention(
            block_query, limits, all_key[None], all_value[None], row_positions, key_block
        )[0]
        return lax.dynamic_update_slice_in_dim(
            memory_now, row_norm(attended).astype(jnp.bfloat16), offset, 0
        )

    memory = lax.fori_loop(
        0, row_total // key_block, fill_block, jnp.zeros((row_total, HDIM), jnp.bfloat16)
    )
    token_piece = token_count // block_count
    own_tokens = (
        device_rows * token_count
        + block_index * token_piece
        + jnp.arange(token_piece, dtype=jnp.int32)[None, :]
    ).reshape(-1)
    own_up = own_up.reshape(1, device_count * token_piece, HDIM)
    result = blocked_attention(
        own_up, own_tokens // SHORT, memory[None], memory[None], row_positions, key_block
    )[0]
    result = result.astype(jnp.bfloat16).reshape(device_count, token_piece, HDIM)
    returned = lax.all_to_all(result, "seq", split_axis=0, concat_axis=0, tiled=True)
    output_heads = returned.reshape(HEADS, token_count, HDIM)
    return jnp.transpose(output_heads, (1, 0, 2)).reshape(token_count, HEADS * HDIM)


NT = (((1,), (1,)), ((), ()))


def attend(queries, keys, values, first_row, tokens_per_row, masked_from):
    scores = lax.dot_general(queries, keys, NT, preferred_element_type=jnp.float32)
    exponent = jnp.exp(scores * (1.0 / math.sqrt(HDIM)))
    last = exponent[:, masked_from:]
    row = lax.broadcasted_iota(jnp.int32, last.shape, 0) + first_row
    key = lax.broadcasted_iota(jnp.int32, last.shape, 1) * tokens_per_row
    last = jnp.where(key <= row, last, 0.0)
    parts = [last]
    if masked_from:
        parts = [exponent[:, :masked_from], last]
    exponent = jnp.concatenate(parts, axis=1) if masked_from else last
    denominator = jnp.sum(exponent, axis=1, keepdims=True)
    numerator = jnp.dot(
        exponent.astype(jnp.bfloat16), values, preferred_element_type=jnp.float32
    )
    return numerator / denominator


def fused_kernel(
    n, team, planes,
    query_hbm, key_hbm, value_hbm, up_hbm, query_gain_hbm, key_gain_hbm, up_gain_hbm,
    out_ref,
    query_src, key_src, value_src, up_query, query_gain, key_gain, up_gain,
    edge_send, edge_recv, up_send, up_recv, qkv_send, qkv_recv, mem, ret_send,
    edge_sems, up_ssem, up_rsem, qkv_ssem, qkv_rsem, mem_ssem, mem_rsem, ret_ssem, ret_rsem,
    local_sems, in_sems,
):
    me = lax.axis_index("seq")
    plane = me // team
    member = me % team
    tokens = query_src.shape[0]
    rows = tokens // SHORT
    block = rows * team

    def remote(src, dst, ssem, rsem, target):
        return pltpu.make_async_remote_copy(
            src_ref=src, dst_ref=dst, send_sem=ssem, recv_sem=rsem,
            device_id={"seq": target}, device_id_type=pl.DeviceIdType.MESH,
        )

    loads = [
        pltpu.make_async_copy(src, dst, in_sems.at[at])
        for at, (src, dst) in enumerate((
            (query_hbm, query_src), (key_hbm, key_src), (value_hbm, value_src),
            (up_hbm, up_query), (query_gain_hbm, query_gain),
            (key_gain_hbm, key_gain), (up_gain_hbm, up_gain),
        ))
    ]
    for load in loads:
        load.start()
    barrier = pltpu.get_barrier_semaphore()

    @pl.loop(1, n)
    def _(k):
        pl.semaphore_signal(
            barrier, inc=1, device_id={"seq": (me + k) % n},
            device_id_type=pl.DeviceIdType.MESH,
        )

    sources = (query_src, key_src, value_src)
    edge_token = lax.broadcasted_iota(jnp.int32, (8, tokens), 1)
    edge_row = lax.broadcasted_iota(jnp.int32, (8, tokens), 0)
    edge = None
    for at, source in enumerate(sources):
        pick = jnp.where(
            (edge_row == at) & (edge_token >= tokens - SHIFT), 1.0 / SHORT, 0.0
        ).astype(jnp.bfloat16)
        loads[at].wait()
        term = jnp.dot(pick, source[...], preferred_element_type=jnp.float32)
        edge = term if edge is None else edge + term
    edge_send[...] = edge
    pl.semaphore_wait(barrier, n - 1)

    edge_copy = remote(
        edge_send, edge_recv, edge_sems.at[0], edge_sems.at[1], lax.min(me + 1, n - 1)
    )

    @pl.when(me < n - 1)
    def _():
        edge_copy.start()

    for load in loads[3:]:
        load.wait()
    for head in range(HEADS):
        cols = slice(head * HDIM, (head + 1) * HDIM)
        part = up_query[:, cols].astype(jnp.float32)
        scale = lax.rsqrt(jnp.mean(part * part, axis=1, keepdims=True) + epsilon)
        up_send[head] = (part * scale * up_gain[head : head + 1]).astype(jnp.bfloat16)

    pool_row = lax.broadcasted_iota(jnp.int32, (rows, tokens), 0) * SHORT
    pool_token = lax.broadcasted_iota(jnp.int32, (rows, tokens), 1)
    pool = jnp.where(
        (pool_token <= pool_row) & (pool_token >= pool_row - SHIFT), 1.0 / SHORT, 0.0
    ).astype(jnp.bfloat16)
    pooled_all = [
        jnp.dot(pool, source[...], preferred_element_type=jnp.float32) for source in sources
    ]

    @pl.when(me == 0)
    def _():
        edge_recv[...] = jnp.zeros_like(edge_recv)

    @pl.when(me > 0)
    def _():
        edge_copy.wait_recv()

    first = lax.broadcasted_iota(jnp.int32, (rows, HDIM), 0) == 0
    for at, (pooled, gain) in enumerate(zip(pooled_all, (query_gain, key_gain, None))):
        for head in range(HEADS):
            cols = slice(head * HDIM, (head + 1) * HDIM)
            part = pooled[:, cols]
            part = part + jnp.where(first, edge_recv[at : at + 1, cols], 0.0)
            if gain is not None:
                scale = lax.rsqrt(jnp.mean(part * part, axis=1, keepdims=True) + epsilon)
                part = part * scale * gain[head : head + 1]
            qkv_send[head, at * rows : (at + 1) * rows] = part.astype(jnp.bfloat16)

    def head_of(device):
        return (device % team) * planes + device // team

    def qkv_copy(target):
        return remote(
            qkv_send.at[head_of(target)], qkv_recv.at[me],
            qkv_ssem.at[target], qkv_rsem.at[me], target,
        )

    for hop in sorted(range(planes), key=lambda hop: -min(hop, planes - hop)):
        target_plane = (plane + hop) % planes

        @pl.loop(0, team)
        def _(k):
            target = target_plane * team + (member + k) % team

            @pl.when(target != me)
            def _():
                qkv_copy(target).start()

    def up_copy(target):
        return remote(
            up_send.at[pl.ds(target * planes, planes)], up_recv.at[member],
            up_ssem.at[target], up_rsem.at[member], plane * team + target,
        )

    @pl.loop(1, team)
    def _(k):
        up_copy((member + k) % team).start()

    own_qkv = pltpu.make_async_copy(
        qkv_send.at[head_of(me)], qkv_recv.at[me], local_sems.at[0]
    )
    own_up = pltpu.make_async_copy(
        up_send.at[pl.ds(member * planes, planes)], up_recv.at[member], local_sems.at[1]
    )
    own_qkv.start()
    own_up.start()
    own_qkv.wait()

    def mem_copy(target, at):
        part = mem.at[plane, at * block : (at + 1) * block]
        return remote(
            part, part, mem_ssem.at[target, at], mem_rsem.at[plane, at],
            target * team + member,
        )

    for at in range(planes):
        for other in range(team):
            source = at * team + other

            @pl.when(source != me)
            def _():
                remote(
                    qkv_send.at[0], qkv_recv.at[source],
                    qkv_ssem.at[source], qkv_rsem.at[source], source,
                ).wait_recv()

        upto = (at + 1) * team
        queries = qkv_recv[at * team : upto, :rows].reshape(block, HDIM)
        keys = qkv_recv[:upto, rows : 2 * rows].reshape(upto * rows, HDIM)
        values = qkv_recv[:upto, 2 * rows :].reshape(upto * rows, HDIM)
        attended = attend(queries, keys, values, 0, 1, at * block)
        mem[plane, at * block : (at + 1) * block] = row_norm(attended).astype(jnp.bfloat16)
        for target in reversed(range(at, planes)):

            @pl.when(target != plane)
            def _():
                mem_copy(target, at).start()

    own_up.wait()

    @pl.loop(1, team)
    def _(k):
        source = (member + k) % team
        remote(
            up_send.at[pl.ds(0, planes)], up_recv.at[source],
            up_ssem.at[source], up_rsem.at[source], plane * team + source,
        ).wait_recv()

    def ret_copy(target, part):
        column = pl.multiple_of((member * planes + part) * HDIM, HDIM)
        return remote(
            ret_send.at[target, part], out_ref.at[:, pl.ds(column, HDIM)],
            ret_ssem.at[target, part], ret_rsem.at[member, part], plane * team + target,
        )

    for here in range(planes):

        @pl.when(plane == here)
        def _():
            count = (here + 1) * block

            @pl.loop(0, planes)
            def _(step):
                part = (here + step) % planes

                @pl.when(part != here)
                def _():
                    for at in range(here + 1):
                        slot = mem.at[part, at * block : (at + 1) * block]
                        remote(
                            slot, slot, mem_ssem.at[part, at], mem_rsem.at[part, at],
                            part * team + member,
                        ).wait_recv()

                memory = mem[part, :count]
                for target in range(team):
                    value = attend(
                        up_recv[target, part], memory, memory,
                        target * tokens, SHORT, here * block,
                    ).astype(jnp.bfloat16)
                    ret_send[target, part] = value

                for target in range(team):

                    @pl.when(target != member)
                    def _():
                        ret_copy(target, part).start()

                column = pl.multiple_of((member * planes + part) * HDIM, HDIM)
                out_ref[:, pl.ds(column, HDIM)] = ret_send[member, part]

    @pl.when(me < n - 1)
    def _():
        edge_copy.wait_send()

    @pl.loop(1, n)
    def _(k):
        qkv_copy((me + k) % n).wait_send()

    @pl.loop(1, team)
    def _(k):
        up_copy((member + k) % team).wait_send()

    for at in range(planes):
        for target in range(at, planes):

            @pl.when(target != plane)
            def _():
                mem_copy(target, at).wait_send()

    @pl.loop(1, team)
    def _(k):
        other = (member + k) % team
        for part in range(planes):
            ret_copy(other, part).wait_send()
            column = pl.multiple_of((other * planes + part) * HDIM, HDIM)
            remote(
                ret_send.at[other, part], out_ref.at[:, pl.ds(column, HDIM)],
                ret_ssem.at[other, part], ret_rsem.at[other, part], plane * team + other,
            ).wait_recv()


def local_fused(query_src, key_src, value_src, up_query, query_gain, key_gain, up_gain):
    n = lax.axis_size("seq")
    team = math.isqrt(n)
    planes = n // team
    tokens, width = query_src.shape
    rows = tokens // SHORT
    bf16, dma = jnp.bfloat16, pltpu.SemaphoreType.DMA
    return pl.pallas_call(
        functools.partial(fused_kernel, n, team, planes),
        out_shape=jax.ShapeDtypeStruct((tokens, width), bf16),
        in_specs=[pl.BlockSpec(memory_space=pltpu.HBM)] * 7,
        out_specs=pl.BlockSpec(memory_space=pltpu.VMEM),
        scratch_shapes=[pltpu.VMEM((tokens, width), bf16)] * 4
        + [pltpu.VMEM((HEADS, HDIM), jnp.float32)] * 3
        + [
            pltpu.VMEM((8, width), jnp.float32),
            pltpu.VMEM((8, width), jnp.float32),
            pltpu.VMEM((HEADS, tokens, HDIM), bf16),
            pltpu.VMEM((team, planes, tokens, HDIM), bf16),
            pltpu.VMEM((HEADS, 3 * rows, HDIM), bf16),
            pltpu.VMEM((n, 3 * rows, HDIM), bf16),
            pltpu.VMEM((planes, n * rows, HDIM), bf16),
            pltpu.VMEM((team, planes, tokens, HDIM), bf16),
            dma((2,)),
            dma((team,)),
            dma((team,)),
            dma((n,)),
            dma((n,)),
            dma((planes, planes)),
            dma((planes, planes)),
            dma((team, planes)),
            dma((team, planes)),
            dma((2,)),
            dma((7,)),
        ],
        compiler_params=pltpu.CompilerParams(
            collective_id=0, has_side_effects=True, vmem_limit_bytes=60 * 1024 * 1024
        ),
    )(
        query_src, key_src, value_src, up_query,
        *(gain.reshape(HEADS, HDIM) for gain in (query_gain, key_gain, up_gain)),
    )


def local(query_src, *others):
    n = lax.axis_size("seq")
    square = math.isqrt(n) ** 2 == n
    whole_tiles = query_src.shape[0] % (16 * SHORT) == 0
    if n == HEADS and square and whole_tiles:
        return local_fused(query_src, *others)
    return local_general(query_src, *others)


def solution(mesh):
    in_specs = (
        P(("groups", "seq"), None),
        P(("groups", "seq"), None),
        P(("groups", "seq"), None),
        P(("groups", "seq"), None),
        P(),
        P(),
        P(),
    )
    out_specs = P(("groups", "seq"), None)
    return jax.shard_map(local, mesh=mesh, in_specs=in_specs, out_specs=out_specs, check_vma=False)
```

```python
import functools
import math

import jax
import jax.numpy as jnp
from jax import lax
from jax.experimental import pallas as pl
from jax.experimental.pallas import tpu as pltpu
from jax.sharding import PartitionSpec as P

HEADS = 16
HDIM = 128
SHORT = 4
SHIFT = 3


epsilon = 1e-06


def shifted(value, axis, steps):
    count = lax.axis_size(axis)
    leading, last = (max(0, -steps), min(count, count - steps))
    return lax.ppermute(value, axis, [(source, source + steps) for source in range(leading, last)])


def head_norm(values, gain_vector):
    row_count = values.shape[0]
    by_head = values.reshape(row_count, HEADS, HDIM)
    inverse_rms = lax.rsqrt(jnp.mean(by_head * by_head, axis=2, keepdims=True) + epsilon)
    return (by_head * inverse_rms * gain_vector.reshape(1, HEADS, HDIM)).reshape(
        row_count, HEADS * HDIM
    )


def row_norm(values):
    return values * lax.rsqrt(jnp.mean(values * values, axis=-1, keepdims=True) + epsilon)


def pooled_rows(source, edge_rows):
    widened = jnp.concatenate([edge_rows, source[: source.shape[0] - SHIFT]], axis=0).astype(
        jnp.float32
    )
    return jnp.mean(widened.reshape(-1, SHORT, widened.shape[1]), axis=1)


def blocked_attention(queries, query_limit, key_rows, value_rows, key_positions, block_size):
    head_count, query_count, head_size = queries.shape
    block_total = key_rows.shape[1] // block_size
    ceiling = jnp.max(query_limit)

    def visit_block(block_index, totals):
        offset = block_index * block_size
        block_pos = lax.dynamic_slice_in_dim(key_positions, offset, block_size, 0)

        def compute(state):
            numer_in, denom_in = state
            key_block = lax.dynamic_slice_in_dim(key_rows, offset, block_size, 1)
            value_block = lax.dynamic_slice_in_dim(value_rows, offset, block_size, 1)
            scores = jnp.einsum(
                "hqd,hkd->hqk", queries, key_block, preferred_element_type=jnp.float32
            ) / math.sqrt(HDIM)
            visible = block_pos[None, :] <= query_limit[:, None]
            exponent = jnp.where(visible[None], jnp.exp(scores), 0.0)
            denom_out = denom_in + jnp.sum(exponent, axis=2)
            numer_out = numer_in + jnp.einsum(
                "hqk,hkd->hqd",
                exponent.astype(jnp.bfloat16),
                value_block,
                preferred_element_type=jnp.float32,
            )
            return (numer_out, denom_out)

        return lax.cond(jnp.min(block_pos) <= ceiling, compute, lambda state: state, totals)

    initial = (
        jnp.zeros((head_count, query_count, head_size), jnp.float32),
        jnp.zeros((head_count, query_count), jnp.float32),
    )
    numerator, denominator = lax.fori_loop(0, block_total, visit_block, initial)
    return numerator / denominator[:, :, None]


def spread_heads(matrices, row_count, block_count, device_count):
    count = len(matrices)
    joined = jnp.stack(matrices).reshape(count, row_count, HEADS, HDIM)
    joined = jnp.transpose(joined, (2, 0, 1, 3)).reshape(HEADS, 1, count * row_count, HDIM)
    return jnp.broadcast_to(joined, (HEADS, block_count, count * row_count, HDIM)).reshape(
        device_count, count * row_count, HDIM
    )


def split_pieces(matrix, row_count, block_count, device_count):
    piece = row_count // block_count
    parted = matrix.reshape(block_count, piece, HEADS, HDIM)
    return jnp.transpose(parted, (2, 0, 1, 3)).reshape(device_count, piece, HDIM)


def local_general(query_src, key_src, value_src, up_query, query_gain, key_gain, up_gain):
    device_count = lax.axis_size("seq")
    device_index = lax.axis_index("seq")
    block_count = device_count // HEADS
    block_index = device_index % block_count
    token_count = query_src.shape[0]
    edges = jnp.stack(
        [
            query_src[token_count - SHIFT :],
            key_src[token_count - SHIFT :],
            value_src[token_count - SHIFT :],
        ]
    )
    edges = shifted(edges, "seq", 1)
    short_query = head_norm(pooled_rows(query_src, edges[0]), query_gain).astype(jnp.bfloat16)
    short_key = head_norm(pooled_rows(key_src, edges[1]), key_gain).astype(jnp.bfloat16)
    short_value = pooled_rows(value_src, edges[2]).astype(jnp.bfloat16)
    row_count = short_query.shape[0]
    up_heads = head_norm(up_query.astype(jnp.float32), up_gain).astype(jnp.bfloat16)
    row_total = row_count * device_count
    key_block = math.gcd(512, row_total)
    row_positions = jnp.arange(row_total, dtype=jnp.int32)
    device_rows = jnp.arange(device_count, dtype=jnp.int32)[:, None]
    qkv_out = spread_heads(
        [short_query, short_key, short_value], row_count, block_count, device_count
    )
    up_out = split_pieces(up_heads, token_count, block_count, device_count)
    arrived, own_up = (
        lax.all_to_all(qkv_out, "seq", split_axis=0, concat_axis=0, tiled=True),
        lax.all_to_all(up_out, "seq", split_axis=0, concat_axis=0, tiled=True),
    )
    all_query = arrived[:, :row_count].reshape(row_total, HDIM)
    all_key = arrived[:, row_count : 2 * row_count].reshape(row_total, HDIM)
    all_value = arrived[:, 2 * row_count :].reshape(row_total, HDIM)

    def fill_block(index_now, memory_now):
        offset = index_now * key_block
        block_query = lax.dynamic_slice_in_dim(all_query, offset, key_block, 0)[None]
        limits = offset + jnp.arange(key_block, dtype=jnp.int32)
        attended = blocked_attention(
            block_query, limits, all_key[None], all_value[None], row_positions, key_block
        )[0]
        return lax.dynamic_update_slice_in_dim(
            memory_now, row_norm(attended).astype(jnp.bfloat16), offset, 0
        )

    memory = lax.fori_loop(
        0, row_total // key_block, fill_block, jnp.zeros((row_total, HDIM), jnp.bfloat16)
    )
    token_piece = token_count // block_count
    own_tokens = (
        device_rows * token_count
        + block_index * token_piece
        + jnp.arange(token_piece, dtype=jnp.int32)[None, :]
    ).reshape(-1)
    own_up = own_up.reshape(1, device_count * token_piece, HDIM)
    result = blocked_attention(
        own_up, own_tokens // SHORT, memory[None], memory[None], row_positions, key_block
    )[0]
    result = result.astype(jnp.bfloat16).reshape(device_count, token_piece, HDIM)
    returned = lax.all_to_all(result, "seq", split_axis=0, concat_axis=0, tiled=True)
    output_heads = returned.reshape(HEADS, token_count, HDIM)
    return jnp.transpose(output_heads, (1, 0, 2)).reshape(token_count, HEADS * HDIM)


NT = (((1,), (1,)), ((), ()))


def attend(queries, keys, values, first_row, tokens_per_row, masked_from):
    scores = lax.dot_general(queries, keys, NT, preferred_element_type=jnp.float32)
    exponent = jnp.exp(scores * (1.0 / math.sqrt(HDIM)))
    last = exponent[:, masked_from:]
    row = lax.broadcasted_iota(jnp.int32, last.shape, 0) + first_row
    key = lax.broadcasted_iota(jnp.int32, last.shape, 1) * tokens_per_row
    last = jnp.where(key <= row, last, 0.0)
    parts = [last]
    if masked_from:
        parts = [exponent[:, :masked_from], last]
    exponent = jnp.concatenate(parts, axis=1) if masked_from else last
    denominator = jnp.sum(exponent, axis=1, keepdims=True)
    numerator = jnp.dot(
        exponent.astype(jnp.bfloat16), values, preferred_element_type=jnp.float32
    )
    return numerator / denominator


def fused_kernel(
    n, team, planes,
    query_hbm, key_hbm, value_hbm, up_hbm, query_gain_hbm, key_gain_hbm, up_gain_hbm,
    out_ref,
    query_src, key_src, value_src, up_query, query_gain, key_gain, up_gain,
    edge_send, edge_recv, up_send, up_recv, qkv_send, qkv_recv, mem, ret_send,
    edge_sems, up_ssem, up_rsem, qkv_ssem, qkv_rsem, mem_ssem, mem_rsem, ret_ssem, ret_rsem,
    local_sems, in_sems,
):
    me = lax.axis_index("seq")
    plane = me // team
    member = me % team
    tokens = query_src.shape[0]
    rows = tokens // SHORT
    block = rows * team

    def remote(src, dst, ssem, rsem, target):
        return pltpu.make_async_remote_copy(
            src_ref=src, dst_ref=dst, send_sem=ssem, recv_sem=rsem,
            device_id={"seq": target}, device_id_type=pl.DeviceIdType.MESH,
        )

    loads = [
        pltpu.make_async_copy(src, dst, in_sems.at[at])
        for at, (src, dst) in enumerate((
            (query_hbm, query_src), (key_hbm, key_src), (value_hbm, value_src),
            (up_hbm, up_query), (query_gain_hbm, query_gain),
            (key_gain_hbm, key_gain), (up_gain_hbm, up_gain),
        ))
    ]
    for load in loads:
        load.start()
    barrier = pltpu.get_barrier_semaphore()

    @pl.loop(1, n)
    def _(k):
        pl.semaphore_signal(
            barrier, inc=1, device_id={"seq": (me + k) % n},
            device_id_type=pl.DeviceIdType.MESH,
        )

    sources = (query_src, key_src, value_src)
    edge_token = lax.broadcasted_iota(jnp.int32, (8, tokens), 1)
    edge_row = lax.broadcasted_iota(jnp.int32, (8, tokens), 0)
    edge = None
    for at, source in enumerate(sources):
        pick = jnp.where(
            (edge_row == at) & (edge_token >= tokens - SHIFT), 1.0 / SHORT, 0.0
        ).astype(jnp.bfloat16)
        loads[at].wait()
        term = jnp.dot(pick, source[...], preferred_element_type=jnp.float32)
        edge = term if edge is None else edge + term
    edge_send[...] = edge
    pl.semaphore_wait(barrier, n - 1)

    edge_copy = remote(
        edge_send, edge_recv, edge_sems.at[0], edge_sems.at[1], lax.min(me + 1, n - 1)
    )

    @pl.when(me < n - 1)
    def _():
        edge_copy.start()

    for load in loads[3:]:
        load.wait()
    for head in range(HEADS):
        cols = slice(head * HDIM, (head + 1) * HDIM)
        part = up_query[:, cols].astype(jnp.float32)
        scale = lax.rsqrt(jnp.mean(part * part, axis=1, keepdims=True) + epsilon)
        up_send[head] = (part * scale * up_gain[head : head + 1]).astype(jnp.bfloat16)

    pool_row = lax.broadcasted_iota(jnp.int32, (rows, tokens), 0) * SHORT
    pool_token = lax.broadcasted_iota(jnp.int32, (rows, tokens), 1)
    pool = jnp.where(
        (pool_token <= pool_row) & (pool_token >= pool_row - SHIFT), 1.0 / SHORT, 0.0
    ).astype(jnp.bfloat16)
    pooled_all = [
        jnp.dot(pool, source[...], preferred_element_type=jnp.float32) for source in sources
    ]

    @pl.when(me == 0)
    def _():
        edge_recv[...] = jnp.zeros_like(edge_recv)

    @pl.when(me > 0)
    def _():
        edge_copy.wait_recv()

    first = lax.broadcasted_iota(jnp.int32, (rows, HDIM), 0) == 0
    for at, (pooled, gain) in enumerate(zip(pooled_all, (query_gain, key_gain, None))):
        for head in range(HEADS):
            cols = slice(head * HDIM, (head + 1) * HDIM)
            part = pooled[:, cols]
            part = part + jnp.where(first, edge_recv[at : at + 1, cols], 0.0)
            if gain is not None:
                scale = lax.rsqrt(jnp.mean(part * part, axis=1, keepdims=True) + epsilon)
                part = part * scale * gain[head : head + 1]
            qkv_send[head, at * rows : (at + 1) * rows] = part.astype(jnp.bfloat16)

    def head_of(device):
        return (device % team) * planes + device // team

    def qkv_copy(target):
        return remote(
            qkv_send.at[head_of(target)], qkv_recv.at[me],
            qkv_ssem.at[target], qkv_rsem.at[me], target,
        )

    for hop in sorted(range(planes), key=lambda hop: -min(hop, planes - hop)):
        target_plane = (plane + hop) % planes

        @pl.loop(0, team)
        def _(k):
            target = target_plane * team + (member + k) % team

            @pl.when(target != me)
            def _():
                qkv_copy(target).start()

    def up_copy(target):
        return remote(
            up_send.at[pl.ds(target * planes, planes)], up_recv.at[member],
            up_ssem.at[target], up_rsem.at[member], plane * team + target,
        )

    @pl.loop(1, team)
    def _(k):
        up_copy((member + k) % team).start()

    own_qkv = pltpu.make_async_copy(
        qkv_send.at[head_of(me)], qkv_recv.at[me], local_sems.at[0]
    )
    own_up = pltpu.make_async_copy(
        up_send.at[pl.ds(member * planes, planes)], up_recv.at[member], local_sems.at[1]
    )
    own_qkv.start()
    own_up.start()
    own_qkv.wait()

    def mem_copy(target, at):
        part = mem.at[plane, at * block : (at + 1) * block]
        return remote(
            part, part, mem_ssem.at[target, at], mem_rsem.at[plane, at],
            target * team + member,
        )

    for at in range(planes):
        for other in range(team):
            source = at * team + other

            @pl.when(source != me)
            def _():
                remote(
                    qkv_send.at[0], qkv_recv.at[source],
                    qkv_ssem.at[source], qkv_rsem.at[source], source,
                ).wait_recv()

        upto = (at + 1) * team
        queries = qkv_recv[at * team : upto, :rows].reshape(block, HDIM)
        keys = qkv_recv[:upto, rows : 2 * rows].reshape(upto * rows, HDIM)
        values = qkv_recv[:upto, 2 * rows :].reshape(upto * rows, HDIM)
        attended = attend(queries, keys, values, 0, 1, at * block)
        mem[plane, at * block : (at + 1) * block] = row_norm(attended).astype(jnp.bfloat16)
        for target in reversed(range(at, planes)):

            @pl.when(target != plane)
            def _():
                mem_copy(target, at).start()

    own_up.wait()

    @pl.loop(1, team)
    def _(k):
        source = (member + k) % team
        remote(
            up_send.at[pl.ds(0, planes)], up_recv.at[source],
            up_ssem.at[source], up_rsem.at[source], plane * team + source,
        ).wait_recv()

    def ret_copy(target, part):
        column = pl.multiple_of((member * planes + part) * HDIM, HDIM)
        return remote(
            ret_send.at[target, part], out_ref.at[:, pl.ds(column, HDIM)],
            ret_ssem.at[target, part], ret_rsem.at[member, part], plane * team + target,
        )

    for here in range(planes):

        @pl.when(plane == here)
        def _():
            count = (here + 1) * block

            @pl.loop(0, planes)
            def _(step):
                part = (here + step) % planes

                @pl.when(part != here)
                def _():
                    for at in range(here + 1):
                        slot = mem.at[part, at * block : (at + 1) * block]
                        remote(
                            slot, slot, mem_ssem.at[part, at], mem_rsem.at[part, at],
                            part * team + member,
                        ).wait_recv()

                memory = mem[part, :count]
                for target in range(team):
                    value = attend(
                        up_recv[target, part], memory, memory,
                        target * tokens, SHORT, here * block,
                    ).astype(jnp.bfloat16)
                    ret_send[target, part] = value

                for target in range(team):

                    @pl.when(target != member)
                    def _():
                        ret_copy(target, part).start()

                column = pl.multiple_of((member * planes + part) * HDIM, HDIM)
                out_ref[:, pl.ds(column, HDIM)] = ret_send[member, part]

    @pl.when(me < n - 1)
    def _():
        edge_copy.wait_send()

    @pl.loop(1, n)
    def _(k):
        qkv_copy((me + k) % n).wait_send()

    @pl.loop(1, team)
    def _(k):
        up_copy((member + k) % team).wait_send()

    for at in range(planes):
        for target in range(at, planes):

            @pl.when(target != plane)
            def _():
                mem_copy(target, at).wait_send()

    @pl.loop(1, team)
    def _(k):
        other = (member + k) % team
        for part in range(planes):
            ret_copy(other, part).wait_send()
            column = pl.multiple_of((other * planes + part) * HDIM, HDIM)
            remote(
                ret_send.at[other, part], out_ref.at[:, pl.ds(column, HDIM)],
                ret_ssem.at[other, part], ret_rsem.at[other, part], plane * team + other,
            ).wait_recv()


def local_fused(query_src, key_src, value_src, up_query, query_gain, key_gain, up_gain):
    n = lax.axis_size("seq")
    team = n // 2
    planes = n // team
    tokens, width = query_src.shape
    rows = tokens // SHORT
    bf16, dma = jnp.bfloat16, pltpu.SemaphoreType.DMA
    return pl.pallas_call(
        functools.partial(fused_kernel, n, team, planes),
        out_shape=jax.ShapeDtypeStruct((tokens, width), bf16),
        in_specs=[pl.BlockSpec(memory_space=pltpu.HBM)] * 7,
        out_specs=pl.BlockSpec(memory_space=pltpu.VMEM),
        scratch_shapes=[pltpu.VMEM((tokens, width), bf16)] * 4
        + [pltpu.VMEM((HEADS, HDIM), jnp.float32)] * 3
        + [
            pltpu.VMEM((8, width), jnp.float32),
            pltpu.VMEM((8, width), jnp.float32),
            pltpu.VMEM((HEADS, tokens, HDIM), bf16),
            pltpu.VMEM((team, planes, tokens, HDIM), bf16),
            pltpu.VMEM((HEADS, 3 * rows, HDIM), bf16),
            pltpu.VMEM((n, 3 * rows, HDIM), bf16),
            pltpu.VMEM((planes, n * rows, HDIM), bf16),
            pltpu.VMEM((team, planes, tokens, HDIM), bf16),
            dma((2,)),
            dma((team,)),
            dma((team,)),
            dma((n,)),
            dma((n,)),
            dma((planes, planes)),
            dma((planes, planes)),
            dma((team, planes)),
            dma((team, planes)),
            dma((2,)),
            dma((7,)),
        ],
        compiler_params=pltpu.CompilerParams(
            collective_id=0, has_side_effects=True, vmem_limit_bytes=60 * 1024 * 1024
        ),
    )(
        query_src, key_src, value_src, up_query,
        *(gain.reshape(HEADS, HDIM) for gain in (query_gain, key_gain, up_gain)),
    )


def local(query_src, *others):
    n = lax.axis_size("seq")
    paired = n % 2 == 0
    whole_tiles = query_src.shape[0] % (16 * SHORT) == 0
    if n == HEADS and paired and whole_tiles:
        return local_fused(query_src, *others)
    return local_general(query_src, *others)


def solution(mesh):
    in_specs = (
        P(("groups", "seq"), None),
        P(("groups", "seq"), None),
        P(("groups", "seq"), None),
        P(("groups", "seq"), None),
        P(),
        P(),
        P(),
    )
    out_specs = P(("groups", "seq"), None)
    return jax.shard_map(local, mesh=mesh, in_specs=in_specs, out_specs=out_specs, check_vma=False)
```

```python
import functools
import math

import jax
import jax.numpy as jnp
from jax import lax
from jax.experimental import pallas as pl
from jax.experimental.pallas import tpu as pltpu
from jax.sharding import PartitionSpec as P

HEADS = 16
HDIM = 128
SHORT = 4
SHIFT = 3


epsilon = 1e-06


def shifted(value, axis, steps):
    count = lax.axis_size(axis)
    leading, last = (max(0, -steps), min(count, count - steps))
    return lax.ppermute(value, axis, [(source, source + steps) for source in range(leading, last)])


def head_norm(values, gain_vector):
    row_count = values.shape[0]
    by_head = values.reshape(row_count, HEADS, HDIM)
    inverse_rms = lax.rsqrt(jnp.mean(by_head * by_head, axis=2, keepdims=True) + epsilon)
    return (by_head * inverse_rms * gain_vector.reshape(1, HEADS, HDIM)).reshape(
        row_count, HEADS * HDIM
    )


def row_norm(values):
    return values * lax.rsqrt(jnp.mean(values * values, axis=-1, keepdims=True) + epsilon)


def pooled_rows(source, edge_rows):
    widened = jnp.concatenate([edge_rows, source[: source.shape[0] - SHIFT]], axis=0).astype(
        jnp.float32
    )
    return jnp.mean(widened.reshape(-1, SHORT, widened.shape[1]), axis=1)


def blocked_attention(queries, query_limit, key_rows, value_rows, key_positions, block_size):
    head_count, query_count, head_size = queries.shape
    block_total = key_rows.shape[1] // block_size
    ceiling = jnp.max(query_limit)

    def visit_block(block_index, totals):
        offset = block_index * block_size
        block_pos = lax.dynamic_slice_in_dim(key_positions, offset, block_size, 0)

        def compute(state):
            numer_in, denom_in = state
            key_block = lax.dynamic_slice_in_dim(key_rows, offset, block_size, 1)
            value_block = lax.dynamic_slice_in_dim(value_rows, offset, block_size, 1)
            scores = jnp.einsum(
                "hqd,hkd->hqk", queries, key_block, preferred_element_type=jnp.float32
            ) / math.sqrt(HDIM)
            visible = block_pos[None, :] <= query_limit[:, None]
            exponent = jnp.where(visible[None], jnp.exp(scores), 0.0)
            denom_out = denom_in + jnp.sum(exponent, axis=2)
            numer_out = numer_in + jnp.einsum(
                "hqk,hkd->hqd",
                exponent.astype(jnp.bfloat16),
                value_block,
                preferred_element_type=jnp.float32,
            )
            return (numer_out, denom_out)

        return lax.cond(jnp.min(block_pos) <= ceiling, compute, lambda state: state, totals)

    initial = (
        jnp.zeros((head_count, query_count, head_size), jnp.float32),
        jnp.zeros((head_count, query_count), jnp.float32),
    )
    numerator, denominator = lax.fori_loop(0, block_total, visit_block, initial)
    return numerator / denominator[:, :, None]


def spread_heads(matrices, row_count, block_count, device_count):
    count = len(matrices)
    joined = jnp.stack(matrices).reshape(count, row_count, HEADS, HDIM)
    joined = jnp.transpose(joined, (2, 0, 1, 3)).reshape(HEADS, 1, count * row_count, HDIM)
    return jnp.broadcast_to(joined, (HEADS, block_count, count * row_count, HDIM)).reshape(
        device_count, count * row_count, HDIM
    )


def split_pieces(matrix, row_count, block_count, device_count):
    piece = row_count // block_count
    parted = matrix.reshape(block_count, piece, HEADS, HDIM)
    return jnp.transpose(parted, (2, 0, 1, 3)).reshape(device_count, piece, HDIM)


def local_general(query_src, key_src, value_src, up_query, query_gain, key_gain, up_gain):
    device_count = lax.axis_size("seq")
    device_index = lax.axis_index("seq")
    block_count = device_count // HEADS
    block_index = device_index % block_count
    token_count = query_src.shape[0]
    edges = jnp.stack(
        [
            query_src[token_count - SHIFT :],
            key_src[token_count - SHIFT :],
            value_src[token_count - SHIFT :],
        ]
    )
    edges = shifted(edges, "seq", 1)
    short_query = head_norm(pooled_rows(query_src, edges[0]), query_gain).astype(jnp.bfloat16)
    short_key = head_norm(pooled_rows(key_src, edges[1]), key_gain).astype(jnp.bfloat16)
    short_value = pooled_rows(value_src, edges[2]).astype(jnp.bfloat16)
    row_count = short_query.shape[0]
    up_heads = head_norm(up_query.astype(jnp.float32), up_gain).astype(jnp.bfloat16)
    row_total = row_count * device_count
    key_block = math.gcd(512, row_total)
    row_positions = jnp.arange(row_total, dtype=jnp.int32)
    device_rows = jnp.arange(device_count, dtype=jnp.int32)[:, None]
    qkv_out = spread_heads(
        [short_query, short_key, short_value], row_count, block_count, device_count
    )
    up_out = split_pieces(up_heads, token_count, block_count, device_count)
    arrived, own_up = (
        lax.all_to_all(qkv_out, "seq", split_axis=0, concat_axis=0, tiled=True),
        lax.all_to_all(up_out, "seq", split_axis=0, concat_axis=0, tiled=True),
    )
    all_query = arrived[:, :row_count].reshape(row_total, HDIM)
    all_key = arrived[:, row_count : 2 * row_count].reshape(row_total, HDIM)
    all_value = arrived[:, 2 * row_count :].reshape(row_total, HDIM)

    def fill_block(index_now, memory_now):
        offset = index_now * key_block
        block_query = lax.dynamic_slice_in_dim(all_query, offset, key_block, 0)[None]
        limits = offset + jnp.arange(key_block, dtype=jnp.int32)
        attended = blocked_attention(
            block_query, limits, all_key[None], all_value[None], row_positions, key_block
        )[0]
        return lax.dynamic_update_slice_in_dim(
            memory_now, row_norm(attended).astype(jnp.bfloat16), offset, 0
        )

    memory = lax.fori_loop(
        0, row_total // key_block, fill_block, jnp.zeros((row_total, HDIM), jnp.bfloat16)
    )
    token_piece = token_count // block_count
    own_tokens = (
        device_rows * token_count
        + block_index * token_piece
        + jnp.arange(token_piece, dtype=jnp.int32)[None, :]
    ).reshape(-1)
    own_up = own_up.reshape(1, device_count * token_piece, HDIM)
    result = blocked_attention(
        own_up, own_tokens // SHORT, memory[None], memory[None], row_positions, key_block
    )[0]
    result = result.astype(jnp.bfloat16).reshape(device_count, token_piece, HDIM)
    returned = lax.all_to_all(result, "seq", split_axis=0, concat_axis=0, tiled=True)
    output_heads = returned.reshape(HEADS, token_count, HDIM)
    return jnp.transpose(output_heads, (1, 0, 2)).reshape(token_count, HEADS * HDIM)


NT = (((1,), (1,)), ((), ()))


def attend(queries, keys, values, first_row, tokens_per_row, masked_from):
    scores = lax.dot_general(queries, keys, NT, preferred_element_type=jnp.float32)
    exponent = jnp.exp(scores * (1.0 / math.sqrt(HDIM)))
    last = exponent[:, masked_from:]
    row = lax.broadcasted_iota(jnp.int32, last.shape, 0) + first_row
    key = lax.broadcasted_iota(jnp.int32, last.shape, 1) * tokens_per_row
    last = jnp.where(key <= row, last, 0.0)
    parts = [last]
    if masked_from:
        parts = [exponent[:, :masked_from], last]
    exponent = jnp.concatenate(parts, axis=1) if masked_from else last
    denominator = jnp.sum(exponent, axis=1, keepdims=True)
    numerator = jnp.dot(
        exponent.astype(jnp.bfloat16), values, preferred_element_type=jnp.float32
    )
    return numerator / denominator


def fused_kernel(
    n, team, planes,
    query_hbm, key_hbm, value_hbm, up_hbm, query_gain_hbm, key_gain_hbm, up_gain_hbm,
    out_ref,
    query_src, key_src, value_src, up_query, query_gain, key_gain, up_gain,
    edge_send, edge_recv, up_send, up_recv, qkv_send, qkv_recv, mem, ret_send,
    edge_sems, up_ssem, up_rsem, qkv_ssem, qkv_rsem, mem_ssem, mem_rsem, ret_ssem, ret_rsem,
    local_sems, in_sems,
):
    me = lax.axis_index("seq")
    plane = me // team
    member = me % team
    tokens = query_src.shape[0]
    rows = tokens // SHORT
    block = rows * team

    def remote(src, dst, ssem, rsem, target):
        return pltpu.make_async_remote_copy(
            src_ref=src, dst_ref=dst, send_sem=ssem, recv_sem=rsem,
            device_id={"seq": target}, device_id_type=pl.DeviceIdType.MESH,
        )

    loads = [
        pltpu.make_async_copy(src, dst, in_sems.at[at])
        for at, (src, dst) in enumerate((
            (query_hbm, query_src), (key_hbm, key_src), (value_hbm, value_src),
            (up_hbm, up_query), (query_gain_hbm, query_gain),
            (key_gain_hbm, key_gain), (up_gain_hbm, up_gain),
        ))
    ]
    for load in loads:
        load.start()
    barrier = pltpu.get_barrier_semaphore()

    @pl.loop(1, n)
    def _(k):
        pl.semaphore_signal(
            barrier, inc=1, device_id={"seq": (me + k) % n},
            device_id_type=pl.DeviceIdType.MESH,
        )

    sources = (query_src, key_src, value_src)
    edge_token = lax.broadcasted_iota(jnp.int32, (8, tokens), 1)
    edge_row = lax.broadcasted_iota(jnp.int32, (8, tokens), 0)
    edge = None
    for at, source in enumerate(sources):
        pick = jnp.where(
            (edge_row == at) & (edge_token >= tokens - SHIFT), 1.0 / SHORT, 0.0
        ).astype(jnp.bfloat16)
        loads[at].wait()
        term = jnp.dot(pick, source[...], preferred_element_type=jnp.float32)
        edge = term if edge is None else edge + term
    edge_send[...] = edge
    pl.semaphore_wait(barrier, n - 1)

    edge_copy = remote(
        edge_send, edge_recv, edge_sems.at[0], edge_sems.at[1], lax.min(me + 1, n - 1)
    )

    @pl.when(me < n - 1)
    def _():
        edge_copy.start()

    for load in loads[3:]:
        load.wait()
    for head in range(HEADS):
        cols = slice(head * HDIM, (head + 1) * HDIM)
        part = up_query[:, cols].astype(jnp.float32)
        scale = lax.rsqrt(jnp.mean(part * part, axis=1, keepdims=True) + epsilon)
        up_send[head] = (part * scale * up_gain[head : head + 1]).astype(jnp.bfloat16)

    pool_row = lax.broadcasted_iota(jnp.int32, (rows, tokens), 0) * SHORT
    pool_token = lax.broadcasted_iota(jnp.int32, (rows, tokens), 1)
    pool = jnp.where(
        (pool_token <= pool_row) & (pool_token >= pool_row - SHIFT), 1.0 / SHORT, 0.0
    ).astype(jnp.bfloat16)
    pooled_all = [
        jnp.dot(pool, source[...], preferred_element_type=jnp.float32) for source in sources
    ]

    @pl.when(me == 0)
    def _():
        edge_recv[...] = jnp.zeros_like(edge_recv)

    @pl.when(me > 0)
    def _():
        edge_copy.wait_recv()

    first = lax.broadcasted_iota(jnp.int32, (rows, HDIM), 0) == 0
    for at, (pooled, gain) in enumerate(zip(pooled_all, (query_gain, key_gain, None))):
        for head in range(HEADS):
            cols = slice(head * HDIM, (head + 1) * HDIM)
            part = pooled[:, cols]
            part = part + jnp.where(first, edge_recv[at : at + 1, cols], 0.0)
            if gain is not None:
                scale = lax.rsqrt(jnp.mean(part * part, axis=1, keepdims=True) + epsilon)
                part = part * scale * gain[head : head + 1]
            qkv_send[head, at * rows : (at + 1) * rows] = part.astype(jnp.bfloat16)

    def head_of(device):
        return (device % team) * planes + device // team

    def qkv_copy(target):
        return remote(
            qkv_send.at[head_of(target)], qkv_recv.at[me],
            qkv_ssem.at[target], qkv_rsem.at[me], target,
        )

    for hop in sorted(range(planes), key=lambda hop: -min(hop, planes - hop)):
        target_plane = (plane + hop) % planes

        @pl.loop(0, team)
        def _(k):
            target = target_plane * team + (member + k) % team

            @pl.when(target != me)
            def _():
                qkv_copy(target).start()

    def up_copy(target):
        return remote(
            up_send.at[pl.ds(target * planes, planes)], up_recv.at[member],
            up_ssem.at[target], up_rsem.at[member], plane * team + target,
        )

    @pl.loop(1, team)
    def _(k):
        up_copy((member + k) % team).start()

    own_qkv = pltpu.make_async_copy(
        qkv_send.at[head_of(me)], qkv_recv.at[me], local_sems.at[0]
    )
    own_up = pltpu.make_async_copy(
        up_send.at[pl.ds(member * planes, planes)], up_recv.at[member], local_sems.at[1]
    )
    own_qkv.start()
    own_up.start()
    own_qkv.wait()

    def mem_copy(target, at):
        part = mem.at[plane, at * block : (at + 1) * block]
        return remote(
            part, part, mem_ssem.at[target, at], mem_rsem.at[plane, at],
            target * team + member,
        )

    for at in range(planes):
        for other in range(team):
            source = at * team + other

            @pl.when(source != me)
            def _():
                remote(
                    qkv_send.at[0], qkv_recv.at[source],
                    qkv_ssem.at[source], qkv_rsem.at[source], source,
                ).wait_recv()

        upto = (at + 1) * team
        queries = qkv_recv[at * team : upto, :rows].reshape(block, HDIM)
        keys = qkv_recv[:upto, rows : 2 * rows].reshape(upto * rows, HDIM)
        values = qkv_recv[:upto, 2 * rows :].reshape(upto * rows, HDIM)
        attended = attend(queries, keys, values, 0, 1, at * block)
        mem[plane, at * block : (at + 1) * block] = row_norm(attended).astype(jnp.bfloat16)
        for target in reversed(range(at, planes)):

            @pl.when(target != plane)
            def _():
                mem_copy(target, at).start()

    own_up.wait()

    @pl.loop(1, team)
    def _(k):
        source = (member + k) % team
        remote(
            up_send.at[pl.ds(0, planes)], up_recv.at[source],
            up_ssem.at[source], up_rsem.at[source], plane * team + source,
        ).wait_recv()

    def ret_copy(target, part):
        column = pl.multiple_of((member * planes + part) * HDIM, HDIM)
        return remote(
            ret_send.at[target, part], out_ref.at[:, pl.ds(column, HDIM)],
            ret_ssem.at[target, part], ret_rsem.at[member, part], plane * team + target,
        )

    for here in range(planes):

        @pl.when(plane == here)
        def _():
            count = (here + 1) * block

            @pl.loop(0, planes)
            def _(step):
                part = (here + step) % planes

                @pl.when(part != here)
                def _():
                    for at in range(here + 1):
                        slot = mem.at[part, at * block : (at + 1) * block]
                        remote(
                            slot, slot, mem_ssem.at[part, at], mem_rsem.at[part, at],
                            part * team + member,
                        ).wait_recv()

                memory = mem[part, :count]
                hops = sorted(range(team), key=lambda hop: -min(hop, team - hop))
                for at in range(0, team, team // 2):
                    targets = [(member + hop) % team for hop in hops[at : at + team // 2]]
                    values = [
                        attend(
                            up_recv[target, part], memory, memory,
                            target * tokens, SHORT, here * block,
                        ).astype(jnp.bfloat16)
                        for target in targets
                    ]
                    for hop, target, value in zip(hops[at:], targets, values):
                        if hop:
                            ret_send[target, part] = value
                        else:
                            column = pl.multiple_of((member * planes + part) * HDIM, HDIM)
                            out_ref[:, pl.ds(column, HDIM)] = value
                    for hop, target in zip(hops[at:], targets):
                        if hop:
                            ret_copy(target, part).start()

    @pl.when(me < n - 1)
    def _():
        edge_copy.wait_send()

    @pl.loop(1, n)
    def _(k):
        qkv_copy((me + k) % n).wait_send()

    @pl.loop(1, team)
    def _(k):
        up_copy((member + k) % team).wait_send()

    for at in range(planes):
        for target in range(at, planes):

            @pl.when(target != plane)
            def _():
                mem_copy(target, at).wait_send()

    @pl.loop(1, team)
    def _(k):
        other = (member + k) % team
        for part in range(planes):
            ret_copy(other, part).wait_send()
            column = pl.multiple_of((other * planes + part) * HDIM, HDIM)
            remote(
                ret_send.at[other, part], out_ref.at[:, pl.ds(column, HDIM)],
                ret_ssem.at[other, part], ret_rsem.at[other, part], plane * team + other,
            ).wait_recv()


def local_fused(query_src, key_src, value_src, up_query, query_gain, key_gain, up_gain):
    n = lax.axis_size("seq")
    team = n // 2
    planes = n // team
    tokens, width = query_src.shape
    rows = tokens // SHORT
    bf16, dma = jnp.bfloat16, pltpu.SemaphoreType.DMA
    return pl.pallas_call(
        functools.partial(fused_kernel, n, team, planes),
        out_shape=jax.ShapeDtypeStruct((tokens, width), bf16),
        in_specs=[pl.BlockSpec(memory_space=pltpu.HBM)] * 7,
        out_specs=pl.BlockSpec(memory_space=pltpu.VMEM),
        scratch_shapes=[pltpu.VMEM((tokens, width), bf16)] * 4
        + [pltpu.VMEM((HEADS, HDIM), jnp.float32)] * 3
        + [
            pltpu.VMEM((8, width), jnp.float32),
            pltpu.VMEM((8, width), jnp.float32),
            pltpu.VMEM((HEADS, tokens, HDIM), bf16),
            pltpu.VMEM((team, planes, tokens, HDIM), bf16),
            pltpu.VMEM((HEADS, 3 * rows, HDIM), bf16),
            pltpu.VMEM((n, 3 * rows, HDIM), bf16),
            pltpu.VMEM((planes, n * rows, HDIM), bf16),
            pltpu.VMEM((team, planes, tokens, HDIM), bf16),
            dma((2,)),
            dma((team,)),
            dma((team,)),
            dma((n,)),
            dma((n,)),
            dma((planes, planes)),
            dma((planes, planes)),
            dma((team, planes)),
            dma((team, planes)),
            dma((2,)),
            dma((7,)),
        ],
        compiler_params=pltpu.CompilerParams(
            collective_id=0, has_side_effects=True, vmem_limit_bytes=60 * 1024 * 1024
        ),
    )(
        query_src, key_src, value_src, up_query,
        *(gain.reshape(HEADS, HDIM) for gain in (query_gain, key_gain, up_gain)),
    )


def local(query_src, *others):
    n = lax.axis_size("seq")
    paired = n % 2 == 0
    whole_tiles = query_src.shape[0] % (16 * SHORT) == 0
    if n == HEADS and paired and whole_tiles:
        return local_fused(query_src, *others)
    return local_general(query_src, *others)


def solution(mesh):
    in_specs = (
        P(("groups", "seq"), None),
        P(("groups", "seq"), None),
        P(("groups", "seq"), None),
        P(("groups", "seq"), None),
        P(),
        P(),
        P(),
    )
    out_specs = P(("groups", "seq"), None)
    return jax.shard_map(local, mesh=mesh, in_specs=in_specs, out_specs=out_specs, check_vma=False)
```
